32 devices in a mesh: sess: 4 (over y, x), exp: 8 (over z, core).
Axes of the slice: x: 2, y: 2, z: 4, core: 2. Of those that a mesh axis runs over, the one named last changes fastest.
Arguments:
- tokens: bfloat16 [1024, 2048], P(('sess', 'exp')), may hold values from -6 to 6
- thinker_gain: float32 [2048], replicated, may hold values from 0.25 to 1.75
- thinker_ids: int32 [1024, 8], P(('sess', 'exp')), may hold values from 0 to 7, all different within a row; in each aligned block of 32 rows (0 to 31, 32 to 63, ...) at most 32 rows name the same one
- thinker_gates: float32 [1024, 8], P(('sess', 'exp')), may hold values from 0.05 to 0.25
- w_gate: bfloat16 [8, 2048, 768], P('exp'), may hold values from -0.125 to 0.125
- w_up: bfloat16 [8, 2048, 768], P('exp'), may hold values from -0.125 to 0.125
- w_down: bfloat16 [8, 768, 2048], P('exp'), may hold values from -0.21875 to 0.21875
- talker_in: bfloat16 [1024, 1024], P(('sess', 'exp')), may hold values from -6 to 6
- talker_gain: float32 [1024], replicated, may hold values from 0.25 to 1.75
- talker_ids: int32 [1024, 2], P(('sess', 'exp')), may hold values from 0 to 3, all different within a row; in each aligned block of 32 rows (0 to 31, 32 to 63, ...) at most 32 rows name the same one
- talker_gates: float32 [1024, 2], P(('sess', 'exp')), may hold values from 0.2 to 0.6
- t_gate: bfloat16 [4, 1024, 384], P('sess'), may hold values from -0.1875 to 0.1875
- t_up: bfloat16 [4, 1024, 384], P('sess'), may hold values from -0.1875 to 0.1875
- t_down: bfloat16 [4, 384, 1024], P('sess'), may hold values from -0.3125 to 0.3125
- conv_state: float32 [1024, 3, 1024], P(('sess', 'exp')), may hold values from -6 to 6
- conv_kernel: float32 [4, 1024], replicated, may hold values from -3 to 3
- conv_gain: float32 [1024], replicated, may hold values from 0.25 to 1.75
Outputs:
- thought: bfloat16 [1024, 2048], P(('sess', 'exp'))
- spoken: bfloat16 [1024, 1024], P(('sess', 'exp'))
- audio_frame: bfloat16 [1024, 1024], P(('sess', 'exp'))
- new_state: float32 [1024, 3, 1024], P(('sess', 'exp'))
The draws below stay inside these ranges and needn't reach their ends.
Inputs may be any that keep to these rules, and one draw needn't show every extreme that they name: `thinker_ids`: each row names 8 different experts; within the 32 rows of one device no expert is named by more than 32 rows. `talker_ids`: each row names 2 different experts; within the 32 rows of one device no expert is named by more than 32 rows.
All inputs are finite; a program needn't handle non-finite values.
Results may differ from the reference program's by a relative error of at most 0.0055.
Values may be sent and summed in bfloat16 or wider, within the bound.
A program may use at most 64 MiB of HBM per device.

```python
import math
import jax
import jax.numpy as jnp
import numpy as np
from jax import lax

D = 2048
FF = 768
TOP = 8
DT = 1024
FT = 384
TTOP = 2
KW = 4
SESS_DEV = 32
EXPERTS = 8
TEXP = 4
SESSIONS = 1024
CAP = 32
CAPT = 32


def shard_levels(own_key, shape, split, least, top_value):
    level, own = 1.0, jax.random.fold_in(own_key, 6)
    for dim, parts in split:
        steps = jnp.exp(jax.random.uniform(jax.random.fold_in(own, dim), (parts,), jnp.float32, least / len(split), top_value / len(split)))
        level = level * jnp.repeat(steps, shape[dim] // parts).reshape([-1 if axis == dim else 1 for axis in range(len(shape))])
    return level


def deal_out(key, own, number, rows, count, top, limit, slope):
    sequence = jax.random.permutation(key, count)
    heavy_load, ordinary = shares(count, rows * top, limit, slope, True), shares(count, rows * top, limit, slope, False)
    places = jnp.arange(count)

    def named(tallies, turn):
        used = int((tallies > 0).sum())
        fixed = max(1, used // 4)
        passed = fixed + (places - fixed + turn * (used - fixed)) % max(1, count - fixed)
        return jnp.zeros((count,), jnp.int32).at[sequence[jnp.where(places < fixed, places, passed)]].set(jnp.asarray(tallies, jnp.int32))

    tallies = jnp.where(number % 4 == 0, named(heavy_load, number // 4), named(ordinary, number - number // 4 - 1))
    mixed = jax.random.permutation(jax.random.fold_in(own, 3), count)
    donor, receiver = mixed[0:count // 2 * 2:2], mixed[1:count // 2 * 2:2]
    room = jnp.minimum(tallies[donor] - 1, limit - tallies[receiver]) // 2
    room = jnp.where((donor == sequence[0]) | (receiver == sequence[0]) | (tallies[receiver] == 0), 0, jnp.maximum(room, 0))
    passed = jax.random.randint(jax.random.fold_in(own, 4), (count // 2,), 0, 1 << 20) % (room + 1)
    tallies = tallies.at[donor].add(-passed).at[receiver].add(passed)
    items = jnp.searchsorted(jnp.cumsum(tallies), jnp.arange(rows * top), side="right").astype(jnp.int32)
    grid = items.reshape(top, rows).T
    grid = grid[jax.random.permutation(jax.random.fold_in(own, 1), rows)]
    turn = jax.random.randint(jax.random.fold_in(own, 2), (rows, 1), 0, top)
    return jnp.take_along_axis(grid, (jnp.arange(top)[None, :] + turn) % top, axis=1)


def shares(number_of, total, bound, slope, full):
    loads = [(1 << 20) // math.isqrt(grade ** slope) + 1 for grade in range(1, number_of + 1)]
    largest = bound if full else min(bound, max(-(-total // number_of), total * loads[0] // sum(loads)))
    least = 1 if total - largest >= number_of - 1 else 0
    holding, rest = [largest] + [least] * (number_of - 1), total - largest - least * (number_of - 1)
    while rest > 0:
        free = [i for i in range(1, number_of) if holding[i] < largest] or [i for i in range(1, number_of) if holding[i] < bound]
        whole, remaining = sum([loads[i] for i in free]), rest
        for i in free:
            addition = min(bound - holding[i], max(1, remaining * loads[i] // whole), rest)
            holding[i] = holding[i] + addition
            rest = rest - addition
    return np.array(holding)


def noise(rng, dims, scale, most, shards=(), held_as=jnp.bfloat16):
    array = jax.random.normal(rng, dims, jnp.float32) * scale
    if len(shards) > 0:
        array = shard_levels(rng, dims, shards, -0.22, 0.18) * array
    return jnp.clip(array, min=-most, max=most).astype(held_as)


def setup_inputs(seed: int = 0) -> dict:
    seeds = jax.random.split(jax.random.key(seed), 18)
    tokens = noise(seeds[0], (SESSIONS, D), 1.0, 6.0, ((0, 32),))
    thinker_gain = jnp.clip(1.0 + 0.15 * jax.random.normal(seeds[1], (D,), jnp.float32), 0.25, 1.75)
    thinker_ids_keys = jax.random.split(jax.random.fold_in(seeds[2], 1), SESSIONS // SESS_DEV)
    thinker_ids_turns = jax.random.permutation(jax.random.fold_in(seeds[2], 3), SESSIONS // SESS_DEV)
    thinker_ids = jax.vmap(lambda own, number: deal_out(jax.random.fold_in(seeds[2], 2), own, number, SESS_DEV, EXPERTS, TOP, CAP, 2))(thinker_ids_keys, thinker_ids_turns).reshape((SESSIONS, TOP))
    thinker_gates = jnp.clip(0.05 + 0.2 * jax.random.uniform(seeds[3], (SESSIONS, TOP), jnp.float32) ** shard_levels(seeds[3], (SESSIONS, TOP), ((0, 32),), -0.2, 0.2), 0.05, 0.25)
    w_gate = noise(seeds[4], (EXPERTS, D, FF), D ** -0.5, 0.125, ((0, 8),))
    w_up = noise(seeds[5], (EXPERTS, D, FF), D ** -0.5, 0.125, ((0, 8),))
    w_down = noise(seeds[6], (EXPERTS, FF, D), FF ** -0.5, 0.21875, ((0, 8),))
    talker_in = noise(seeds[7], (SESSIONS, DT), 1.0, 6.0, ((0, 32),))
    talker_gain = jnp.clip(1.0 + 0.15 * jax.random.normal(seeds[8], (DT,), jnp.float32), 0.25, 1.75)
    talker_ids_keys = jax.random.split(jax.random.fold_in(seeds[9], 1), SESSIONS // SESS_DEV)
    talker_ids_turns = jax.random.permutation(jax.random.fold_in(seeds[9], 3), SESSIONS // SESS_DEV)
    talker_ids = jax.vmap(lambda own, number: deal_out(jax.random.fold_in(seeds[9], 2), own, number, SESS_DEV, TEXP, TTOP, CAPT, 2))(talker_ids_keys, talker_ids_turns).reshape((SESSIONS, TTOP))
    talker_gates = jnp.clip(0.2 + 0.400000021 * jax.random.uniform(seeds[10], (SESSIONS, TTOP), jnp.float32) ** shard_levels(seeds[10], (SESSIONS, TTOP), ((0, 32),), -0.2, 0.2), 0.2, 0.6)
    t_gate = noise(seeds[11], (TEXP, DT, FT), DT ** -0.5, 0.1875, ((0, 4),))
    t_up = noise(seeds[12], (TEXP, DT, FT), DT ** -0.5, 0.1875, ((0, 4),))
    t_down = noise(seeds[13], (TEXP, FT, DT), FT ** -0.5, 0.3125, ((0, 4),))
    conv_state = noise(seeds[14], (SESSIONS, KW - 1, DT), 1.0, 6.0, ((0, 32),), jnp.float32)
    conv_kernel = noise(seeds[15], (KW, DT), 0.5, 3.0, (), jnp.float32)
    conv_gain = jnp.clip(1.0 + 0.15 * jax.random.normal(seeds[16], (DT,), jnp.float32), 0.25, 1.75)
    return dict(tokens=tokens, thinker_gain=thinker_gain, thinker_ids=thinker_ids, thinker_gates=thinker_gates, w_gate=w_gate, w_up=w_up, w_down=w_down, talker_in=talker_in, talker_gain=talker_gain, talker_ids=talker_ids, talker_gates=talker_gates, t_gate=t_gate, t_up=t_up, t_down=t_down, conv_state=conv_state, conv_kernel=conv_kernel, conv_gain=conv_gain)


def rms_scale(values, gain):
    wide = values.astype(jnp.float32)
    scale = lax.rsqrt(lax.optimization_barrier(jnp.mean(wide * wide, axis=-1, keepdims=True)) + 1e-06)
    return (wide * scale * gain).astype(jnp.bfloat16)

def bucket_slots(ids, count):
    onehot = (ids[:, :, None] == jnp.arange(count, dtype=jnp.int32)).astype(jnp.int32)
    used = lax.optimization_barrier(jnp.sum(onehot, axis=1, dtype=jnp.int32))
    before = jnp.cumsum(used, axis=0, dtype=jnp.int32) - used
    return lax.optimization_barrier(jnp.sum(onehot * before[:, None, :], axis=2, dtype=jnp.int32))

def expert_rows(rows, weight_gate, weight_up, weight_down):
    gate = jnp.dot(rows, weight_gate, preferred_element_type=jnp.float32)
    up = jnp.dot(rows, weight_up, preferred_element_type=jnp.float32)
    hidden = (jax.nn.silu(gate) * up).astype(jnp.bfloat16)
    return jnp.dot(hidden, weight_down, preferred_element_type=jnp.float32).astype(jnp.bfloat16)

def moe_layer(values, gain, ids, gates, weight_gate, weight_up, weight_down, count, capacity, blocks):
    sessions = values.shape[0]
    per_block = sessions // blocks
    normed = rms_scale(values, gain)
    slots = jax.vmap(lambda group: bucket_slots(group, count))(ids.reshape(blocks, per_block, -1))
    slots = slots.reshape(ids.shape)
    block_of = (jnp.arange(sessions, dtype=jnp.int32) // per_block)[:, None]
    places = block_of * capacity + slots
    rows_all = blocks * capacity

    def visit(expert, total):
        chosen = ids == expert
        has_any = jnp.any(chosen, axis=1)
        where_row = lax.optimization_barrier(jnp.sum(jnp.where(chosen, places, 0), axis=1, dtype=jnp.int32))
        weight = lax.optimization_barrier(jnp.sum(jnp.where(chosen, gates, 0.0), axis=1))
        target = jnp.where(has_any, where_row, rows_all).astype(jnp.int32)
        rows = jnp.zeros((rows_all, values.shape[1]), jnp.bfloat16).at[target].set(normed, mode='drop')
        result = expert_rows(rows, lax.dynamic_index_in_dim(weight_gate, expert, 0, keepdims=False), lax.dynamic_index_in_dim(weight_up, expert, 0, keepdims=False), lax.dynamic_index_in_dim(weight_down, expert, 0, keepdims=False))
        picked = jnp.take(result, where_row, axis=0)
        return total + weight[:, None] * picked.astype(jnp.float32)
    total = lax.fori_loop(0, count, visit, jnp.zeros(values.shape, jnp.float32))
    return (values.astype(jnp.float32) + total).astype(jnp.bfloat16)

def reference(tokens, thinker_gain, thinker_ids, thinker_gates, w_gate, w_up, w_down, talker_in, talker_gain, talker_ids, talker_gates, t_gate, t_up, t_down, conv_state, conv_kernel, conv_gain):
    blocks = SESSIONS // SESS_DEV
    thought = moe_layer(tokens, thinker_gain, thinker_ids, thinker_gates, w_gate, w_up, w_down, EXPERTS, CAP, blocks)
    spoken = moe_layer(talker_in, talker_gain, talker_ids, talker_gates, t_gate, t_up, t_down, TEXP, CAPT, blocks)
    window = jnp.concatenate([conv_state, spoken.astype(jnp.float32)[:, None, :]], axis=1)
    mixed = lax.optimization_barrier(jnp.sum(window * conv_kernel[None, :, :], axis=1))
    scale = lax.rsqrt(lax.optimization_barrier(jnp.mean(mixed * mixed, axis=-1, keepdims=True)) + 1e-06)
    audio_frame = (mixed * scale * conv_gain).astype(jnp.bfloat16)
    new_state = window[:, 1:, :]
    return (thought, spoken, audio_frame, new_state)
```

```python
import functools

import jax
import jax.numpy as jnp
from jax import lax
from jax.experimental import pallas as pl
from jax.experimental.pallas import tpu as pltpu
from jax.sharding import PartitionSpec as P

MESH = pl.DeviceIdType.MESH
CORES = 2


def rms_scale(values, gain):
    wide = values.astype(jnp.float32)
    scale = lax.rsqrt(jnp.mean(wide * wide, axis=-1, keepdims=True) + 1e-06)
    return (wide * scale * gain).astype(jnp.bfloat16)


def gate_table(ids, gates, count, width):
    sessions = ids.shape[1]
    row = lax.broadcasted_iota(jnp.int32, (width, sessions), 0)
    expert = jnp.where(row < count, row, row - count)
    table = jnp.zeros((width, sessions), jnp.float32)
    for k in range(ids.shape[0]):
        table = table + jnp.where(expert == ids[k : k + 1, :], gates[k : k + 1, :], 0.0)
    table = jnp.where(row < 2 * count, table, 0.0)
    high = table.astype(jnp.bfloat16)
    low = (table - high.astype(jnp.float32)).astype(jnp.bfloat16)
    parts = jnp.where(row < count, high.astype(jnp.float32), low.astype(jnp.float32))
    here = lax.broadcasted_iota(jnp.int32, (sessions, sessions), 0)
    there = lax.broadcasted_iota(jnp.int32, (sessions, sessions), 1)
    eye = (here == there).astype(jnp.bfloat16)
    return lax.dot_general(
        eye,
        parts.astype(jnp.bfloat16),
        (((1,), (1,)), ((), ())),
        preferred_element_type=jnp.float32,
    )


def gate_column(table, expert, count):
    lane = lax.broadcasted_iota(jnp.int32, table.shape, 1)
    chosen = (lane == expert) | (lane == expert + count)
    return jnp.sum(jnp.where(chosen, table, 0.0), axis=1, keepdims=True)


def hidden_units(rows, gate_weight, up_weight):
    gate = jnp.dot(rows, gate_weight, preferred_element_type=jnp.float32)
    up = jnp.dot(rows, up_weight, preferred_element_type=jnp.float32)
    return (jax.nn.silu(gate) * up).astype(jnp.bfloat16)


def kernel(
    n,
    m,
    tokens,
    gain,
    ids,
    gates,
    w_gate,
    w_up,
    w_down,
    talker_in,
    talker_gain,
    talker_ids,
    talker_gates,
    t_gate,
    t_up,
    t_down,
    conv_state,
    conv_kernel,
    conv_gain,
    thought,
    spoken,
    audio,
    new_state,
    held,
    part,
    sib_out,
    sib_in,
    ret_out,
    ret_in,
    total,
    talk_held,
    talk_out,
    talk_in,
    wg,
    wu,
    wd,
    tg,
    tu,
    td,
    state,
    w_sem,
    held_recv,
    up_send,
    down_send,
    side_send,
    sib_send,
    sib_recv,
    ret_send,
    ret_recv,
    talk_send,
    talk_recv,
    back_send,
    back_recv,
):
    me = lax.axis_index("exp")
    ms = lax.axis_index("sess")
    chips = n // CORES
    z = me // CORES
    c = lax.rem(me, CORES)
    sibling = z * CORES + 1 - c
    sessions, depth = tokens.shape
    width = held.shape[2] - depth

    loads = [
        pltpu.make_async_copy(src, dst, w_sem.at[i])
        for i, (src, dst) in enumerate(
            (
                (w_gate.at[0], wg),
                (w_up.at[0], wu),
                (w_down.at[0], wd),
                (t_gate.at[0], tg),
                (t_up.at[0], tu),
                (t_down.at[0], td),
                (conv_state, state),
            )
        )
    ]
    for load in loads:
        load.start()

    barrier = pltpu.get_barrier_semaphore()
    pl.semaphore_signal(barrier, inc=1, device_id={"exp": sibling}, device_id_type=MESH)
    for k in range(1, chips):
        other = lax.rem(z + k, chips) * CORES + c
        pl.semaphore_signal(barrier, inc=1, device_id={"exp": other}, device_id_type=MESH)
    for k in range(1, m):
        pl.semaphore_signal(barrier, inc=1, device_id={"sess": lax.rem(ms + k, m)}, device_id_type=MESH)

    held[me, :, :depth] = rms_scale(tokens[...], gain[...])
    held[me, :, depth:] = gate_table(ids[...], gates[...], n, width).astype(jnp.bfloat16)
    talk_held[ms] = rms_scale(talker_in[...], talker_gain[...])
    pl.semaphore_wait(barrier, chips + m - 1)

    def pass_on(slot, send_sem, target):
        return pltpu.make_async_remote_copy(
            src_ref=held.at[slot],
            dst_ref=held.at[slot],
            send_sem=send_sem,
            recv_sem=held_recv.at[slot],
            device_id={"exp": target},
            device_id_type=MESH,
        )

    def upward(chip):
        return pass_on(chip * CORES + c, up_send.at[chip], lax.rem(me + CORES, n))

    def downward(chip):
        return pass_on(chip * CORES + c, down_send.at[chip], lax.rem(me + n - CORES, n))

    def sideways(chip):
        return pass_on(chip * CORES + c, side_send.at[chip], sibling)

    def talk_copy(source, target, send_sem, recv_sem, peer, k):
        return pltpu.make_async_remote_copy(
            src_ref=source,
            dst_ref=target,
            send_sem=send_sem.at[k],
            recv_sem=recv_sem.at[ms],
            device_id={"sess": peer},
            device_id_type=MESH,
        )

    def arrival(buffer, recv_sem, slot):
        pltpu.make_async_copy(buffer.at[slot], buffer.at[slot], recv_sem.at[slot]).wait()

    def sib_copy(chip):
        return pltpu.make_async_remote_copy(
            src_ref=sib_out.at[chip],
            dst_ref=sib_in.at[chip],
            send_sem=sib_send.at[chip],
            recv_sem=sib_recv.at[chip],
            device_id={"exp": sibling},
            device_id_type=MESH,
        )

    def ret_copy(chip):
        return pltpu.make_async_remote_copy(
            src_ref=ret_out.at[chip],
            dst_ref=ret_in.at[z],
            send_sem=ret_send.at[chip],
            recv_sem=ret_recv.at[z],
            device_id={"exp": chip * CORES + c},
            device_id_type=MESH,
        )

    @pl.when(z + 1 < chips)
    def _():
        upward(z).start()

    @pl.when(z > 0)
    def _():
        downward(z).start()

    sideways(z).start()
    for k in range(1, m):
        talk_copy(talk_held.at[ms], talk_held.at[ms], talk_send, talk_recv, lax.rem(ms + k, m), k).start()

    def compute(chip):
        rows = held[pl.ds(chip * CORES, CORES)].reshape(CORES * sessions, depth + width)
        column = gate_column(rows[:, depth:].astype(jnp.float32), me, n)
        hidden = hidden_units(rows[:, :depth], wg[...], wu[...])
        step = min(512, depth)
        for at in range(0, depth, step):
            out = jnp.dot(hidden, wd[:, at : at + step], preferred_element_type=jnp.float32)
            part[:, :, at : at + step] = (out * column).reshape(CORES, sessions, step)
        sib_out[chip] = part[1 - c].astype(jnp.bfloat16)
        sib_copy(chip).start()

    def order(k):
        both = jnp.minimum(z, chips - 1 - z)
        near = (k + 1) // 2
        paired = jnp.where(lax.rem(k, 2) == 1, z - near, z + near)
        single = jnp.where(z < chips - 1 - z, z + k - both, z - k + both)
        return jnp.where(k <= 2 * both, paired, single)

    for load in loads[:3]:
        load.wait()
    arrival(held, held_recv, sibling)
    compute(z)
    total[...] = tokens[...].astype(jnp.float32) + part[c]

    def step(k, carry):
        chip = order(k)
        arrival(held, held_recv, chip * CORES + c)

        @pl.when((chip < z) & (z + 1 < chips))
        def _():
            upward(chip).start()

        @pl.when((chip > z) & (z > 0))
        def _():
            downward(chip).start()

        sideways(chip).start()
        before = order(k - 1)
        finish(before)
        arrival(held, held_recv, chip * CORES + 1 - c)
        compute(chip)
        ret_out[chip] = part[c].astype(jnp.bfloat16)
        return carry

    def finish(chip):
        arrival(sib_in, sib_recv, chip)

        @pl.when(chip == z)
        def _():
            total[...] = total[...] + sib_in[chip].astype(jnp.float32)

        @pl.when(chip != z)
        def _():
            ret_out[chip] = (ret_out[chip].astype(jnp.float32) + sib_in[chip].astype(jnp.float32)).astype(jnp.bfloat16)
            ret_copy(chip).start()

    lax.fori_loop(1, chips, step, 0)
    finish(order(chips - 1))

    for load in loads[3:6]:
        load.wait()
    for k in range(1, m):
        arrival(talk_held, talk_recv, lax.rem(ms + k, m))
    talk_depth = talker_in.shape[1]
    rows = talk_held[...].reshape(m * sessions, talk_depth)
    hidden = hidden_units(rows, tg[...], tu[...])
    out = jnp.dot(hidden, td[...], preferred_element_type=jnp.float32)
    talk_out[...] = out.astype(jnp.bfloat16).reshape(m, sessions, talk_depth)
    for k in range(1, m):
        peer = lax.rem(ms + k, m)
        talk_copy(talk_out.at[peer], talk_in.at[ms], back_send, back_recv, peer, k).start()
    talk_in[ms] = talk_out[ms]
    table = gate_table(talker_ids[...], talker_gates[...], m, 128 * (-(-2 * m // 128)))
    loads[6].wait()
    for k in range(1, m):
        arrival(talk_in, back_recv, lax.rem(ms + k, m))
    said = talker_in[...].astype(jnp.float32)
    for e in range(m):
        said = said + gate_column(table, e, m) * talk_in[e].astype(jnp.float32)
    said = said.astype(jnp.bfloat16)
    spoken[...] = said
    taps = conv_kernel.shape[0]
    newest = said.astype(jnp.float32)
    mixed = newest * conv_kernel[taps - 1 : taps, :]
    for j in range(taps - 1):
        mixed = mixed + state[j] * conv_kernel[j : j + 1, :]
        if j > 0:
            new_state[j - 1] = state[j]
    new_state[taps - 2] = newest
    scale = lax.rsqrt(jnp.mean(mixed * mixed, axis=-1, keepdims=True) + 1e-06)
    audio[...] = (mixed * scale * conv_gain[...]).astype(jnp.bfloat16)

    for k in range(1, chips):
        chip = order(k)
        arrival(ret_in, ret_recv, chip)
        total[...] = total[...] + ret_in[chip].astype(jnp.float32)
    thought[...] = total[...].astype(jnp.bfloat16)

    @pl.when(z + 1 < chips)
    def _():
        upward(z).wait_send()

    @pl.when(z > 0)
    def _():
        downward(z).wait_send()

    sideways(z).wait_send()
    sib_copy(z).wait_send()
    for k in range(1, chips):
        chip = order(k)

        @pl.when((chip < z) & (z + 1 < chips))
        def _():
            upward(chip).wait_send()

        @pl.when((chip > z) & (z > 0))
        def _():
            downward(chip).wait_send()

        sideways(chip).wait_send()
        sib_copy(chip).wait_send()
        ret_copy(chip).wait_send()
    for k in range(1, m):
        peer = lax.rem(ms + k, m)
        talk_copy(talk_held.at[ms], talk_held.at[ms], talk_send, talk_recv, peer, k).wait_send()
        talk_copy(talk_out.at[peer], talk_in.at[ms], back_send, back_recv, peer, k).wait_send()


def shards(
    tokens,
    thinker_gain,
    thinker_ids,
    thinker_gates,
    w_gate,
    w_up,
    w_down,
    talker_in,
    talker_gain,
    talker_ids,
    talker_gates,
    t_gate,
    t_up,
    t_down,
    conv_state,
    conv_kernel,
    conv_gain,
):
    n = lax.axis_size("exp")
    m = lax.axis_size("sess")
    chips = n // CORES
    sessions, depth = tokens.shape
    talk_depth = talker_in.shape[1]
    width = 128 * (-(-2 * n // 128))
    taps = conv_kernel.shape[0]
    half = jnp.bfloat16
    vmem = pl.BlockSpec(memory_space=pltpu.VMEM)
    hbm = pl.BlockSpec(memory_space=pl.ANY)
    dma = pltpu.SemaphoreType.DMA
    thought, spoken, audio, new_state = pl.pallas_call(
        functools.partial(kernel, n, m),
        out_shape=(
            jax.ShapeDtypeStruct((sessions, depth), half),
            jax.ShapeDtypeStruct((sessions, talk_depth), half),
            jax.ShapeDtypeStruct((sessions, talk_depth), half),
            jax.ShapeDtypeStruct((taps - 1, sessions, talk_depth), jnp.float32),
        ),
        in_specs=[vmem, vmem, vmem, vmem, hbm, hbm, hbm, vmem, vmem, vmem, vmem, hbm, hbm, hbm, hbm, vmem, vmem],
        out_specs=(vmem, vmem, vmem, vmem),
        scratch_shapes=[
            pltpu.VMEM((n, sessions, depth + width), half),
            pltpu.VMEM((CORES, sessions, depth), jnp.float32),
            pltpu.VMEM((chips, sessions, depth), half),
            pltpu.VMEM((chips, sessions, depth), half),
            pltpu.VMEM((chips, sessions, depth), half),
            pltpu.VMEM((chips, sessions, depth), half),
            pltpu.VMEM((sessions, depth), jnp.float32),
            pltpu.VMEM((m, sessions, talk_depth), half),
            pltpu.VMEM((m, sessions, talk_depth), half),
            pltpu.VMEM((m, sessions, talk_depth), half),
            pltpu.VMEM(w_gate.shape[1:], half),
            pltpu.VMEM(w_up.shape[1:], half),
            pltpu.VMEM(w_down.shape[1:], half),
            pltpu.VMEM(t_gate.shape[1:], half),
            pltpu.VMEM(t_up.shape[1:], half),
            pltpu.VMEM(t_down.shape[1:], half),
            pltpu.VMEM((taps - 1, sessions, talk_depth), jnp.float32),
            dma((7,)),
            dma((n,)),
            dma((chips,)),
            dma((chips,)),
            dma((chips,)),
            dma((chips,)),
            dma((chips,)),
            dma((chips,)),
            dma((chips,)),
            dma((m,)),
            dma((m,)),
            dma((m,)),
            dma((m,)),
        ],
        compiler_params=pltpu.CompilerParams(
            collective_id=0, has_side_effects=True, vmem_limit_bytes=48 * 1024 * 1024
        ),
    )(
        tokens,
        thinker_gain[None],
        thinker_ids.T,
        thinker_gates.T,
        w_gate,
        w_up,
        w_down,
        talker_in,
        talker_gain[None],
        talker_ids.T,
        talker_gates.T,
        t_gate,
        t_up,
        t_down,
        jnp.transpose(conv_state, (1, 0, 2)),
        conv_kernel,
        conv_gain[None],
    )
    return thought, spoken, audio, jnp.transpose(new_state, (1, 0, 2))


def solution(mesh):
    placed = (
        P(("sess", "exp"), None),
        P(),
        P(("sess", "exp"), None),
        P(("sess", "exp"), None),
        P("exp", None, None),
        P("exp", None, None),
        P("exp", None, None),
        P(("sess", "exp"), None),
        P(),
        P(("sess", "exp"), None),
        P(("sess", "exp"), None),
        P("sess", None, None),
        P("sess", None, None),
        P("sess", None, None),
        P(("sess", "exp"), None, None),
        P(),
        P(),
    )
    return jax.shard_map(
        shards,
        mesh=mesh,
        in_specs=placed,
        out_specs=(
            P(("sess", "exp"), None),
            P(("sess", "exp"), None),
            P(("sess", "exp"), None),
            P(("sess", "exp"), None, None),
        ),
        check_vma=False,
    )
```

```python
import functools

import jax
import jax.numpy as jnp
from jax import lax
from jax.experimental import pallas as pl
from jax.experimental.pallas import tpu as pltpu
from jax.sharding import PartitionSpec as P

MESH = pl.DeviceIdType.MESH
CORES = 2
VMEM = 64 * 1024 * 1024


def rms_scale(values, gain):
    wide = values.astype(jnp.float32)
    scale = lax.rsqrt(jnp.mean(wide * wide, axis=-1, keepdims=True) + 1e-06)
    return (wide * scale * gain).astype(jnp.bfloat16)


def gate_table(ids, gates, count, width):
    sessions = ids.shape[1]
    row = lax.broadcasted_iota(jnp.int32, (width, sessions), 0)
    expert = jnp.where(row < count, row, row - count)
    table = jnp.zeros((width, sessions), jnp.float32)
    for k in range(ids.shape[0]):
        table = table + jnp.where(expert == ids[k : k + 1, :], gates[k : k + 1, :], 0.0)
    table = jnp.where(row < 2 * count, table, 0.0)
    high = table.astype(jnp.bfloat16)
    low = (table - high.astype(jnp.float32)).astype(jnp.bfloat16)
    parts = jnp.where(row < count, high.astype(jnp.float32), low.astype(jnp.float32))
    here = lax.broadcasted_iota(jnp.int32, (sessions, sessions), 0)
    there = lax.broadcasted_iota(jnp.int32, (sessions, sessions), 1)
    eye = (here == there).astype(jnp.bfloat16)
    return lax.dot_general(
        eye,
        parts.astype(jnp.bfloat16),
        (((1,), (1,)), ((), ())),
        preferred_element_type=jnp.float32,
    )


def gate_column(table, expert, count):
    lane = lax.broadcasted_iota(jnp.int32, table.shape, 1)
    chosen = (lane == expert) | (lane == expert + count)
    return jnp.sum(jnp.where(chosen, table, 0.0), axis=1, keepdims=True)


def hidden_units(rows, gate_weight, up_weight):
    gate = jnp.dot(rows, gate_weight, preferred_element_type=jnp.float32)
    up = jnp.dot(rows, up_weight, preferred_element_type=jnp.float32)
    return (jax.nn.silu(gate) * up).astype(jnp.bfloat16)


def kernel(n, m, *refs):
    inputs, refs = refs[:17], refs[17:]
    results, refs = refs[:4], refs[4:]
    (thought, spoken, audio, new_state), out_sem, refs = refs[:4], refs[4], refs[5:]
    local, in_sem, refs = refs[:17], refs[17], refs[18:]
    (held, part, sib_out, sib_in, ret_out, ret_in, total, talk_held, talk_out, talk_in), refs = refs[:10], refs[10:]
    (held_recv, up_send, down_send, side_send, sib_send, sib_recv, ret_send, ret_recv), refs = refs[:8], refs[8:]
    talk_send, talk_recv, back_send, back_recv = refs
    (tokens, gain, ids, gates, wg, wu, wd, talker_in, talker_gain) = local[:9]
    (talker_ids, talker_gates, tg, tu, td, state, conv_kernel, conv_gain) = local[9:]
    me = lax.axis_index("exp")
    ms = lax.axis_index("sess")
    chips = n // CORES
    z = me // CORES
    c = lax.rem(me, CORES)
    sibling = z * CORES + 1 - c
    sessions, depth = tokens.shape
    width = held.shape[2] - depth

    loads = [pltpu.make_async_copy(inputs[i], local[i], in_sem.at[i]) for i in range(17)]
    for i in (0, 1, 2, 3, 7, 8, 4, 5, 6, 11, 12, 13, 9, 10, 15, 16, 14):
        loads[i].start()

    barrier = pltpu.get_barrier_semaphore()
    pl.semaphore_signal(barrier, inc=1, device_id={"exp": sibling}, device_id_type=MESH)
    for k in range(1, chips):
        other = lax.rem(z + k, chips) * CORES + c
        pl.semaphore_signal(barrier, inc=1, device_id={"exp": other}, device_id_type=MESH)
    for k in range(1, m):
        pl.semaphore_signal(barrier, inc=1, device_id={"sess": lax.rem(ms + k, m)}, device_id_type=MESH)

    for i in (0, 1, 2, 3):
        loads[i].wait()
    held[me, :, :depth] = rms_scale(tokens[...], gain[...])
    held[me, :, depth:] = gate_table(ids[...], gates[...], n, width).astype(jnp.bfloat16)
    for i in (7, 8):
        loads[i].wait()
    talk_held[ms] = rms_scale(talker_in[...], talker_gain[...])
    pl.semaphore_wait(barrier, chips + m - 1)

    def pass_on(slot, send_sem, target):
        return pltpu.make_async_remote_copy(
            src_ref=held.at[slot],
            dst_ref=held.at[slot],
            send_sem=send_sem,
            recv_sem=held_recv.at[slot],
            device_id={"exp": target},
            device_id_type=MESH,
        )

    def upward(chip):
        return pass_on(chip * CORES + c, up_send.at[chip], lax.rem(me + CORES, n))

    def downward(chip):
        return pass_on(chip * CORES + c, down_send.at[chip], lax.rem(me + n - CORES, n))

    def sideways(chip):
        return pass_on(chip * CORES + c, side_send.at[chip], sibling)

    def talk_copy(source, target, send_sem, recv_sem, peer, k):
        return pltpu.make_async_remote_copy(
            src_ref=source,
            dst_ref=target,
            send_sem=send_sem.at[k],
            recv_sem=recv_sem.at[ms],
            device_id={"sess": peer},
            device_id_type=MESH,
        )

    def arrival(buffer, recv_sem, slot):
        pltpu.make_async_copy(buffer.at[slot], buffer.at[slot], recv_sem.at[slot]).wait()

    def sib_copy(chip):
        return pltpu.make_async_remote_copy(
            src_ref=sib_out.at[chip],
            dst_ref=sib_in.at[chip],
            send_sem=sib_send.at[chip],
            recv_sem=sib_recv.at[chip],
            device_id={"exp": sibling},
            device_id_type=MESH,
        )

    def ret_copy(chip):
        return pltpu.make_async_remote_copy(
            src_ref=ret_out.at[chip],
            dst_ref=ret_in.at[z],
            send_sem=ret_send.at[chip],
            recv_sem=ret_recv.at[z],
            device_id={"exp": chip * CORES + c},
            device_id_type=MESH,
        )

    @pl.when(z + 1 < chips)
    def _():
        upward(z).start()

    @pl.when(z > 0)
    def _():
        downward(z).start()

    sideways(z).start()
    for k in range(1, m):
        talk_copy(talk_held.at[ms], talk_held.at[ms], talk_send, talk_recv, lax.rem(ms + k, m), k).start()

    def compute(chip):
        rows = held[pl.ds(chip * CORES, CORES)].reshape(CORES * sessions, depth + width)
        column = gate_column(rows[:, depth:].astype(jnp.float32), me, n)
        hidden = hidden_units(rows[:, :depth], wg[...], wu[...])
        step = min(512, depth)
        for at in range(0, depth, step):
            out = jnp.dot(hidden, wd[:, at : at + step], preferred_element_type=jnp.float32)
            part[:, :, at : at + step] = (out * column).reshape(CORES, sessions, step)
        sib_out[chip] = part[1 - c].astype(jnp.bfloat16)
        sib_copy(chip).start()

    toward = jnp.where(2 * z < chips, 1, -1)

    def valid(chip):
        return (chip >= 0) & (chip < chips)

    def forward(s):
        for side in (1, -1):
            chip = z + toward * side * s

            @pl.when(valid(chip))
            def _():
                arrival(held, held_recv, chip * CORES + c)

                @pl.when((chip < z) & (z + 1 < chips))
                def _():
                    upward(chip).start()

                @pl.when((chip > z) & (z > 0))
                def _():
                    downward(chip).start()

                sideways(chip).start()

    def finish(chip):
        arrival(sib_in, sib_recv, chip)
        ret_out[chip] = (part[c] + sib_in[chip].astype(jnp.float32)).astype(jnp.bfloat16)
        ret_copy(chip).start()

    def unit(chip):
        arrival(held, held_recv, chip * CORES + 1 - c)
        compute(chip)

    for i in (4, 5, 6):
        loads[i].wait()
    arrival(held, held_recv, sibling)
    compute(z)
    total[...] = tokens[...].astype(jnp.float32) + part[c]
    forward(1)

    for i in (11, 12, 13):
        loads[i].wait()
    for k in range(1, m):
        arrival(talk_held, talk_recv, lax.rem(ms + k, m))
    talk_depth = talker_in.shape[1]
    rows = talk_held[...].reshape(m * sessions, talk_depth)
    hidden = hidden_units(rows, tg[...], tu[...])
    out = jnp.dot(hidden, td[...], preferred_element_type=jnp.float32)
    talk_out[...] = out.astype(jnp.bfloat16).reshape(m, sessions, talk_depth)
    for k in range(1, m):
        peer = lax.rem(ms + k, m)
        talk_copy(talk_out.at[peer], talk_in.at[ms], back_send, back_recv, peer, k).start()

    def level(s, carry):
        first = z + toward * s
        second = z - toward * s

        @pl.when(valid(first))
        def _():
            unit(first)

        @pl.when(s + 1 < chips)
        def _():
            forward(s + 1)

        @pl.when(valid(first))
        def _():
            finish(first)

        @pl.when(valid(second))
        def _():
            unit(second)
            finish(second)

        return carry

    lax.fori_loop(1, chips, level, 0)
    arrival(sib_in, sib_recv, z)
    total[...] = total[...] + sib_in[z].astype(jnp.float32)

    for i in (9, 10, 14, 15, 16):
        loads[i].wait()
    talk_in[ms] = talk_out[ms]
    table = gate_table(talker_ids[...], talker_gates[...], m, 128 * (-(-2 * m // 128)))
    for k in range(1, m):
        arrival(talk_in, back_recv, lax.rem(ms + k, m))
    said = talker_in[...].astype(jnp.float32)
    for e in range(m):
        said = said + gate_column(table, e, m) * talk_in[e].astype(jnp.float32)
    said = said.astype(jnp.bfloat16)
    spoken[...] = said
    taps = conv_kernel.shape[0]
    newest = said.astype(jnp.float32)
    mixed = newest * conv_kernel[taps - 1 : taps, :]
    for j in range(taps - 1):
        mixed = mixed + state[j] * conv_kernel[j : j + 1, :]
        if j > 0:
            new_state[j - 1] = state[j]
    new_state[taps - 2] = newest
    scale = lax.rsqrt(jnp.mean(mixed * mixed, axis=-1, keepdims=True) + 1e-06)
    audio[...] = (mixed * scale * conv_gain[...]).astype(jnp.bfloat16)
    staged = (thought, spoken, audio, new_state)
    writes = [pltpu.make_async_copy(staged[i], results[i], out_sem.at[i]) for i in range(4)]
    for write in writes[1:]:
        write.start()

    for k in range(1, chips):
        chip = lax.rem(z + k, chips)
        arrival(ret_in, ret_recv, chip)
        total[...] = total[...] + ret_in[chip].astype(jnp.float32)
    thought[...] = total[...].astype(jnp.bfloat16)
    writes[0].start()

    @pl.when(z + 1 < chips)
    def _():
        upward(z).wait_send()

    @pl.when(z > 0)
    def _():
        downward(z).wait_send()

    sideways(z).wait_send()
    sib_copy(z).wait_send()
    for k in range(1, chips):
        chip = lax.rem(z + k, chips)

        @pl.when((chip < z) & (z + 1 < chips))
        def _():
            upward(chip).wait_send()

        @pl.when((chip > z) & (z > 0))
        def _():
            downward(chip).wait_send()

        sideways(chip).wait_send()
        sib_copy(chip).wait_send()
        ret_copy(chip).wait_send()
    for k in range(1, m):
        peer = lax.rem(ms + k, m)
        talk_copy(talk_held.at[ms], talk_held.at[ms], talk_send, talk_recv, peer, k).wait_send()
        talk_copy(talk_out.at[peer], talk_in.at[ms], back_send, back_recv, peer, k).wait_send()
    for write in writes:
        write.wait()


def write_out(*refs):
    count = len(refs) // 2
    copies = [pltpu.make_async_copy(refs[i], refs[count + i], refs[-1].at[i]) for i in range(count)]
    for copy in copies:
        copy.start()
    for copy in copies:
        copy.wait()


def shards(
    tokens,
    thinker_gain,
    thinker_ids,
    thinker_gates,
    w_gate,
    w_up,
    w_down,
    talker_in,
    talker_gain,
    talker_ids,
    talker_gates,
    t_gate,
    t_up,
    t_down,
    conv_state,
    conv_kernel,
    conv_gain,
):
    n = lax.axis_size("exp")
    m = lax.axis_size("sess")
    chips = n // CORES
    sessions, depth = tokens.shape
    talk_depth = talker_in.shape[1]
    width = 128 * (-(-2 * n // 128))
    taps = conv_kernel.shape[0]
    half = jnp.bfloat16
    hbm = pl.BlockSpec(memory_space=pltpu.HBM)
    dma = pltpu.SemaphoreType.DMA
    operands = (
        tokens,
        thinker_gain[None],
        thinker_ids.T,
        thinker_gates.T,
        w_gate[0],
        w_up[0],
        w_down[0],
        talker_in,
        talker_gain[None],
        talker_ids.T,
        talker_gates.T,
        t_gate[0],
        t_up[0],
        t_down[0],
        jnp.transpose(conv_state, (1, 0, 2)),
        conv_kernel,
        conv_gain[None],
    )
    shapes = (
        jax.ShapeDtypeStruct((sessions, depth), half),
        jax.ShapeDtypeStruct((sessions, talk_depth), half),
        jax.ShapeDtypeStruct((sessions, talk_depth), half),
        jax.ShapeDtypeStruct((taps - 1, sessions, talk_depth), jnp.float32),
    )
    results = pl.pallas_call(
        functools.partial(kernel, n, m),
        out_shape=shapes,
        in_specs=[hbm] * len(operands),
        out_specs=tuple(hbm for _ in shapes),
        scratch_shapes=[pltpu.VMEM(x.shape, x.dtype) for x in shapes]
        + [dma((len(shapes),))]
        + [pltpu.VMEM(x.shape, x.dtype) for x in operands]
        + [
            dma((len(operands),)),
            pltpu.VMEM((n, sessions, depth + width), half),
            pltpu.VMEM((CORES, sessions, depth), jnp.float32),
            pltpu.VMEM((chips, sessions, depth), half),
            pltpu.VMEM((chips, sessions, depth), half),
            pltpu.VMEM((chips, sessions, depth), half),
            pltpu.VMEM((chips, sessions, depth), half),
            pltpu.VMEM((sessions, depth), jnp.float32),
            pltpu.VMEM((m, sessions, talk_depth), half),
            pltpu.VMEM((m, sessions, talk_depth), half),
            pltpu.VMEM((m, sessions, talk_depth), half),
            dma((n,)),
            dma((chips,)),
            dma((chips,)),
            dma((chips,)),
            dma((chips,)),
            dma((chips,)),
            dma((chips,)),
            dma((chips,)),
            dma((m,)),
            dma((m,)),
            dma((m,)),
            dma((m,)),
        ],
        compiler_params=pltpu.CompilerParams(
            collective_id=0, has_side_effects=True, vmem_limit_bytes=VMEM
        ),
    )(*operands)
    thought, spoken, audio, new_state = pl.pallas_call(
        write_out,
        out_shape=shapes,
        in_specs=[hbm] * len(shapes),
        out_specs=tuple(hbm for _ in shapes),
        scratch_shapes=[dma((len(shapes),))],
        compiler_params=pltpu.CompilerParams(vmem_limit_bytes=VMEM),
    )(*results)
    return thought, spoken, audio, jnp.transpose(new_state, (1, 0, 2))


def solution(mesh):
    placed = (
        P(("sess", "exp"), None),
        P(),
        P(("sess", "exp"), None),
        P(("sess", "exp"), None),
        P("exp", None, None),
        P("exp", None, None),
        P("exp", None, None),
        P(("sess", "exp"), None),
        P(),
        P(("sess", "exp"), None),
        P(("sess", "exp"), None),
        P("sess", None, None),
        P("sess", None, None),
        P("sess", None, None),
        P(("sess", "exp"), None, None),
        P(),
        P(),
    )
    return jax.shard_map(
        shards,
        mesh=mesh,
        in_specs=placed,
        out_specs=(
            P(("sess", "exp"), None),
            P(("sess", "exp"), None),
            P(("sess", "exp"), None),
            P(("sess", "exp"), None, None),
        ),
        check_vma=False,
    )
```

```python
import functools

import jax
import jax.numpy as jnp
from jax import lax
from jax.experimental import pallas as pl
from jax.experimental.pallas import tpu as pltpu
from jax.sharding import PartitionSpec as P

MESH = pl.DeviceIdType.MESH
CORES = 2
VMEM = 64 * 1024 * 1024


def rms_scale(values, gain):
    wide = values.astype(jnp.float32)
    scale = lax.rsqrt(jnp.mean(wide * wide, axis=-1, keepdims=True) + 1e-06)
    return (wide * scale * gain).astype(jnp.bfloat16)


def gate_table(ids, gates, count, width):
    sessions = ids.shape[1]
    row = lax.broadcasted_iota(jnp.int32, (width, sessions), 0)
    expert = jnp.where(row < count, row, row - count)
    table = jnp.zeros((width, sessions), jnp.float32)
    for k in range(ids.shape[0]):
        table = table + jnp.where(expert == ids[k : k + 1, :], gates[k : k + 1, :], 0.0)
    table = jnp.where(row < 2 * count, table, 0.0)
    high = table.astype(jnp.bfloat16)
    low = (table - high.astype(jnp.float32)).astype(jnp.bfloat16)
    parts = jnp.where(row < count, high.astype(jnp.float32), low.astype(jnp.float32))
    here = lax.broadcasted_iota(jnp.int32, (sessions, sessions), 0)
    there = lax.broadcasted_iota(jnp.int32, (sessions, sessions), 1)
    eye = (here == there).astype(jnp.bfloat16)
    return lax.dot_general(
        eye,
        parts.astype(jnp.bfloat16),
        (((1,), (1,)), ((), ())),
        preferred_element_type=jnp.float32,
    )


def gate_column(table, expert, count):
    lane = lax.broadcasted_iota(jnp.int32, table.shape, 1)
    chosen = (lane == expert) | (lane == expert + count)
    return jnp.sum(jnp.where(chosen, table, 0.0), axis=1, keepdims=True)


def hidden_units(rows, gate_weight, up_weight):
    gate = jnp.dot(rows, gate_weight, preferred_element_type=jnp.float32)
    up = jnp.dot(rows, up_weight, preferred_element_type=jnp.float32)
    return (jax.nn.silu(gate) * up).astype(jnp.bfloat16)


def kernel(n, m, *refs):
    inputs, refs = refs[:17], refs[17:]
    results, refs = refs[:4], refs[4:]
    (thought, spoken, audio, new_state), out_sem, refs = refs[:4], refs[4], refs[5:]
    local, in_sem, refs = refs[:17], refs[17], refs[18:]
    (held, part, sib_out, sib_in, ret_out, ret_in, total, talk_held, talk_out, talk_in), refs = refs[:10], refs[10:]
    (held_recv, up_send, down_send, side_send, sib_send, sib_recv, ret_send, ret_recv), refs = refs[:8], refs[8:]
    talk_send, talk_recv, back_send, back_recv = refs
    (tokens, gain, ids, gates, wg, wu, wd, talker_in, talker_gain) = local[:9]
    (talker_ids, talker_gates, tg, tu, td, state, conv_kernel, conv_gain) = local[9:]
    me = lax.axis_index("exp")
    ms = lax.axis_index("sess")
    chips = n // CORES
    z = me // CORES
    c = lax.rem(me, CORES)
    sibling = z * CORES + 1 - c
    sessions, depth = tokens.shape
    width = held.shape[2] - depth

    loads = [pltpu.make_async_copy(inputs[i], local[i], in_sem.at[i]) for i in range(17)]
    for i in (0, 1, 2, 3, 7, 8, 4, 5, 6, 11, 12, 13, 9, 10, 15, 16, 14):
        loads[i].start()

    barrier = pltpu.get_barrier_semaphore()
    pl.semaphore_signal(barrier, inc=1, device_id={"exp": sibling}, device_id_type=MESH)
    for k in range(1, chips):
        other = lax.rem(z + k, chips) * CORES + c
        pl.semaphore_signal(barrier, inc=1, device_id={"exp": other}, device_id_type=MESH)
    for k in range(1, m):
        pl.semaphore_signal(barrier, inc=1, device_id={"sess": lax.rem(ms + k, m)}, device_id_type=MESH)

    for i in (0, 1, 2, 3):
        loads[i].wait()
    held[me, :, :depth] = rms_scale(tokens[...], gain[...])
    held[me, :, depth:] = gate_table(ids[...], gates[...], n, width).astype(jnp.bfloat16)
    for i in (7, 8):
        loads[i].wait()
    talk_held[ms] = rms_scale(talker_in[...], talker_gain[...])
    pl.semaphore_wait(barrier, chips + m - 1)

    def pass_on(slot, send_sem, target):
        return pltpu.make_async_remote_copy(
            src_ref=held.at[slot],
            dst_ref=held.at[slot],
            send_sem=send_sem,
            recv_sem=held_recv.at[slot],
            device_id={"exp": target},
            device_id_type=MESH,
        )

    def upward(chip):
        return pass_on(chip * CORES + c, up_send.at[chip], lax.rem(me + CORES, n))

    def downward(chip):
        return pass_on(chip * CORES + c, down_send.at[chip], lax.rem(me + n - CORES, n))

    def sideways(chip):
        return pass_on(chip * CORES + c, side_send.at[chip], sibling)

    def talk_copy(source, target, send_sem, recv_sem, peer, k):
        return pltpu.make_async_remote_copy(
            src_ref=source,
            dst_ref=target,
            send_sem=send_sem.at[k],
            recv_sem=recv_sem.at[ms],
            device_id={"sess": peer},
            device_id_type=MESH,
        )

    def arrival(buffer, recv_sem, slot):
        pltpu.make_async_copy(buffer.at[slot], buffer.at[slot], recv_sem.at[slot]).wait()

    def sib_copy(chip):
        return pltpu.make_async_remote_copy(
            src_ref=sib_out.at[chip],
            dst_ref=sib_in.at[chip],
            send_sem=sib_send.at[chip],
            recv_sem=sib_recv.at[chip],
            device_id={"exp": sibling},
            device_id_type=MESH,
        )

    def ret_copy(chip):
        return pltpu.make_async_remote_copy(
            src_ref=ret_out.at[chip],
            dst_ref=ret_in.at[z],
            send_sem=ret_send.at[chip],
            recv_sem=ret_recv.at[z],
            device_id={"exp": chip * CORES + c},
            device_id_type=MESH,
        )

    @pl.when(z + 1 < chips)
    def _():
        upward(z).start()

    @pl.when(z > 0)
    def _():
        downward(z).start()

    sideways(z).start()
    for k in range(1, m):
        talk_copy(talk_held.at[ms], talk_held.at[ms], talk_send, talk_recv, lax.rem(ms + k, m), k).start()

    both = jnp.minimum(z, chips - 1 - z)
    middle = both > 0

    def order(k):
        near = (k + 1) // 2
        paired = jnp.where(lax.rem(k, 2) == 1, z - near, z + near)
        single = jnp.where(z < chips - 1 - z, z + k - both, z - k + both)
        return jnp.where(k <= 2 * both, paired, single)

    def forward(k):
        chip = order(k)
        arrival(held, held_recv, chip * CORES + c)

        @pl.when((chip < z) & (z + 1 < chips))
        def _():
            upward(chip).start()

        @pl.when((chip > z) & (z > 0))
        def _():
            downward(chip).start()

        sideways(chip).start()

    def finish(chip, at):
        arrival(sib_in, sib_recv, chip)
        mine = part[at * CORES + c]
        ret_out[chip] = (mine + sib_in[chip].astype(jnp.float32)).astype(jnp.bfloat16)
        ret_copy(chip).start()

    forward(1)

    @pl.when(middle)
    def _():
        forward(2)

    for i in (11, 12, 13):
        loads[i].wait()
    for k in range(1, m):
        arrival(talk_held, talk_recv, lax.rem(ms + k, m))
    talk_depth = talker_in.shape[1]
    rows = talk_held[...].reshape(m * sessions, talk_depth)
    hidden = hidden_units(rows, tg[...], tu[...])
    out = jnp.dot(hidden, td[...], preferred_element_type=jnp.float32)
    talk_out[...] = out.astype(jnp.bfloat16).reshape(m, sessions, talk_depth)
    for k in range(1, m):
        peer = lax.rem(ms + k, m)
        talk_copy(talk_out.at[peer], talk_in.at[ms], back_send, back_recv, peer, k).start()


    for i in (4, 5, 6):
        loads[i].wait()

    def pair(j, carry):
        first = order(2 * j)
        second = order(2 * j + 1)

        @pl.when(j == 1)
        def _():
            finish(order(1), 1)

        @pl.when(j > 1)
        def _():
            finish(order(2 * j - 2), 0)
            finish(order(2 * j - 1), 1)

        @pl.when((j > 1) | ((j == 1) & jnp.logical_not(middle)))
        def _():
            forward(2 * j)
            forward(2 * j + 1)

        arrival(held, held_recv, first * CORES + 1 - c)
        arrival(held, held_recv, second * CORES + 1 - c)
        rows = jnp.concatenate(
            [held[pl.ds(chip * CORES, CORES)].reshape(CORES * sessions, depth + width) for chip in (first, second)]
        )
        column = gate_column(rows[:, depth:].astype(jnp.float32), me, n)
        hidden = hidden_units(rows[:, :depth], wg[...], wu[...])

        @pl.when((j == 0) & middle)
        def _():
            forward(3)

        span = min(512, depth)
        for at in range(0, depth, span):
            out = jnp.dot(hidden, wd[:, at : at + span], preferred_element_type=jnp.float32)
            part[:, :, at : at + span] = (out * column).reshape(2 * CORES, sessions, span)
        sib_out[first] = part[1 - c].astype(jnp.bfloat16)
        sib_copy(first).start()
        sib_out[second] = part[CORES + 1 - c].astype(jnp.bfloat16)
        sib_copy(second).start()

        @pl.when(j == 0)
        def _():
            total[...] = tokens[...].astype(jnp.float32) + part[c]

        return carry

    pairs = chips // 2
    lax.fori_loop(0, pairs, pair, 0)
    if pairs > 1:
        finish(order(chips - 2), 0)
    finish(order(chips - 1), 1)
    arrival(sib_in, sib_recv, z)
    total[...] = total[...] + sib_in[z].astype(jnp.float32)

    for i in (9, 10, 14, 15, 16):
        loads[i].wait()
    talk_in[ms] = talk_out[ms]
    table = gate_table(talker_ids[...], talker_gates[...], m, 128 * (-(-2 * m // 128)))
    for k in range(1, m):
        arrival(talk_in, back_recv, lax.rem(ms + k, m))
    said = talker_in[...].astype(jnp.float32)
    for e in range(m):
        said = said + gate_column(table, e, m) * talk_in[e].astype(jnp.float32)
    said = said.astype(jnp.bfloat16)
    spoken[...] = said
    taps = conv_kernel.shape[0]
    newest = said.astype(jnp.float32)
    mixed = newest * conv_kernel[taps - 1 : taps, :]
    for j in range(taps - 1):
        mixed = mixed + state[j] * conv_kernel[j : j + 1, :]
        if j > 0:
            new_state[j - 1] = state[j]
    new_state[taps - 2] = newest
    scale = lax.rsqrt(jnp.mean(mixed * mixed, axis=-1, keepdims=True) + 1e-06)
    audio[...] = (mixed * scale * conv_gain[...]).astype(jnp.bfloat16)
    staged = (thought, spoken, audio, new_state)
    writes = [pltpu.make_async_copy(staged[i], results[i], out_sem.at[i]) for i in range(4)]
    for write in writes[1:]:
        write.start()

    for k in range(1, chips):
        chip = lax.rem(z + k, chips)
        arrival(ret_in, ret_recv, chip)
        total[...] = total[...] + ret_in[chip].astype(jnp.float32)
    thought[...] = total[...].astype(jnp.bfloat16)
    writes[0].start()

    @pl.when(z + 1 < chips)
    def _():
        upward(z).wait_send()

    @pl.when(z > 0)
    def _():
        downward(z).wait_send()

    sideways(z).wait_send()
    sib_copy(z).wait_send()
    for k in range(1, chips):
        chip = lax.rem(z + k, chips)

        @pl.when((chip < z) & (z + 1 < chips))
        def _():
            upward(chip).wait_send()

        @pl.when((chip > z) & (z > 0))
        def _():
            downward(chip).wait_send()

        sideways(chip).wait_send()
        sib_copy(chip).wait_send()
        ret_copy(chip).wait_send()
    for k in range(1, m):
        peer = lax.rem(ms + k, m)
        talk_copy(talk_held.at[ms], talk_held.at[ms], talk_send, talk_recv, peer, k).wait_send()
        talk_copy(talk_out.at[peer], talk_in.at[ms], back_send, back_recv, peer, k).wait_send()
    for write in writes:
        write.wait()


def write_out(*refs):
    sources, results, staged, in_sem, out_sem = refs[:4], refs[4:8], refs[8:12], refs[12], refs[13]
    reads = [pltpu.make_async_copy(sources[i], staged[i], in_sem.at[i]) for i in range(4)]
    writes = [pltpu.make_async_copy(staged[i], results[i], out_sem.at[i]) for i in range(4)]
    for read in reads:
        read.start()
    for read, write in zip(reads, writes):
        read.wait()
        write.start()
    for write in writes:
        write.wait()


def shards(
    tokens,
    thinker_gain,
    thinker_ids,
    thinker_gates,
    w_gate,
    w_up,
    w_down,
    talker_in,
    talker_gain,
    talker_ids,
    talker_gates,
    t_gate,
    t_up,
    t_down,
    conv_state,
    conv_kernel,
    conv_gain,
):
    n = lax.axis_size("exp")
    m = lax.axis_size("sess")
    chips = n // CORES
    sessions, depth = tokens.shape
    talk_depth = talker_in.shape[1]
    width = 128 * (-(-2 * n // 128))
    taps = conv_kernel.shape[0]
    half = jnp.bfloat16
    hbm = pl.BlockSpec(memory_space=pltpu.HBM)
    dma = pltpu.SemaphoreType.DMA
    operands = (
        tokens,
        thinker_gain[None],
        thinker_ids.T,
        thinker_gates.T,
        w_gate[0],
        w_up[0],
        w_down[0],
        talker_in,
        talker_gain[None],
        talker_ids.T,
        talker_gates.T,
        t_gate[0],
        t_up[0],
        t_down[0],
        jnp.transpose(conv_state, (1, 0, 2)),
        conv_kernel,
        conv_gain[None],
    )
    shapes = (
        jax.ShapeDtypeStruct((sessions, depth), half),
        jax.ShapeDtypeStruct((sessions, talk_depth), half),
        jax.ShapeDtypeStruct((sessions, talk_depth), half),
        jax.ShapeDtypeStruct((taps - 1, sessions, talk_depth), jnp.float32),
    )
    results = pl.pallas_call(
        functools.partial(kernel, n, m),
        out_shape=shapes,
        in_specs=[hbm] * len(operands),
        out_specs=tuple(hbm for _ in shapes),
        scratch_shapes=[pltpu.VMEM(x.shape, x.dtype) for x in shapes]
        + [dma((len(shapes),))]
        + [pltpu.VMEM(x.shape, x.dtype) for x in operands]
        + [
            dma((len(operands),)),
            pltpu.VMEM((n, sessions, depth + width), half),
            pltpu.VMEM((2 * CORES, sessions, depth), jnp.float32),
            pltpu.VMEM((chips, sessions, depth), half),
            pltpu.VMEM((chips, sessions, depth), half),
            pltpu.VMEM((chips, sessions, depth), half),
            pltpu.VMEM((chips, sessions, depth), half),
            pltpu.VMEM((sessions, depth), jnp.float32),
            pltpu.VMEM((m, sessions, talk_depth), half),
            pltpu.VMEM((m, sessions, talk_depth), half),
            pltpu.VMEM((m, sessions, talk_depth), half),
            dma((n,)),
            dma((chips,)),
            dma((chips,)),
            dma((chips,)),
            dma((chips,)),
            dma((chips,)),
            dma((chips,)),
            dma((chips,)),
            dma((m,)),
            dma((m,)),
            dma((m,)),
            dma((m,)),
        ],
        compiler_params=pltpu.CompilerParams(
            collective_id=0, has_side_effects=True, vmem_limit_bytes=VMEM
        ),
    )(*operands)
    thought, spoken, audio, new_state = pl.pallas_call(
        write_out,
        out_shape=shapes,
        in_specs=[hbm] * len(shapes),
        out_specs=tuple(hbm for _ in shapes),
        scratch_shapes=[pltpu.VMEM(x.shape, x.dtype) for x in shapes] + [dma((4,)), dma((4,))],
        compiler_params=pltpu.CompilerParams(vmem_limit_bytes=VMEM),
    )(*results)
    return thought, spoken, audio, jnp.transpose(new_state, (1, 0, 2))


def solution(mesh):
    placed = (
        P(("sess", "exp"), None),
        P(),
        P(("sess", "exp"), None),
        P(("sess", "exp"), None),
        P("exp", None, None),
        P("exp", None, None),
        P("exp", None, None),
        P(("sess", "exp"), None),
        P(),
        P(("sess", "exp"), None),
        P(("sess", "exp"), None),
        P("sess", None, None),
        P("sess", None, None),
        P("sess", None, None),
        P(("sess", "exp"), None, None),
        P(),
        P(),
    )
    return jax.shard_map(
        shards,
        mesh=mesh,
        in_specs=placed,
        out_specs=(
            P(("sess", "exp"), None),
            P(("sess", "exp"), None),
            P(("sess", "exp"), None),
            P(("sess", "exp"), None, None),
        ),
        check_vma=False,
    )
```
